256 devices in a mesh: dp: 8 (over z), blk: 8 (over y_hi, x), mp: 4 (over y_lo, core).
Axes of the slice: x: 4, y: 4 (y_hi: 2, y_lo: 2; y = y_hi * 2 + y_lo), z: 8, core: 2. Of those that a mesh axis runs over, the one named last changes fastest.
Arguments:
- encoder_query: bfloat16 [8, 2048, 2048], P('dp', 'blk', 'mp'), may hold values from -0.4296875 to 0.4296875
- encoder_keys: bfloat16 [8, 2048, 2048], P('dp', 'blk', 'mp'), may hold values from -0.4296875 to 0.4296875
- encoder_values: bfloat16 [8, 2048, 2048], P('dp', 'blk', 'mp'), may hold values from -1.5 to 1.5
- encoder_output: bfloat16 [8, 2048, 2048], P('dp', 'blk', 'mp'), may hold values from -1.5 to 1.5
- encoder_cotangent: bfloat16 [8, 2048, 2048], P('dp', 'blk', 'mp'), may hold values from -96 to 96
- encoder_totals: float32 [8, 8, 2048], P('dp', 'mp', 'blk'), may hold values from 1024 to 4096
- cross_keys: bfloat16 [8, 2048, 2048], P('dp', 'blk', 'mp'), may hold values from -0.4296875 to 0.4296875
- cross_values: bfloat16 [8, 2048, 2048], P('dp', 'blk', 'mp'), may hold values from -1.5 to 1.5
- decoder_query: bfloat16 [8, 256, 2048], P('dp', None, 'mp'), may hold values from -0.4296875 to 0.4296875
- decoder_output: bfloat16 [8, 256, 2048], P('dp', None, 'mp'), may hold values from -1.5 to 1.5
- decoder_cotangent: bfloat16 [8, 256, 2048], P('dp', None, 'mp'), may hold values from -192 to 192
- decoder_totals: float32 [8, 8, 256], P('dp', 'mp'), may hold values from 1024 to 4096
- encoder_states: bfloat16 [8, 2048, 4096], P('dp', 'blk', 'mp'), may hold values from -0.046875 to 0.046875
Outputs:
- encoder_query_grad: bfloat16 [8, 2048, 2048], P('dp', 'blk', 'mp')
- encoder_key_grad: bfloat16 [8, 2048, 2048], P('dp', 'blk', 'mp')
- encoder_value_grad: bfloat16 [8, 2048, 2048], P('dp', 'blk', 'mp')
- cross_key_grad: bfloat16 [8, 2048, 2048], P('dp', 'blk', 'mp')
- cross_value_grad: bfloat16 [8, 2048, 2048], P('dp', 'blk', 'mp')
- decoder_query_grad: bfloat16 [8, 256, 2048], P('dp', None, 'mp')
- value_weight_grad: float32 [4096, 2048], P(('dp', 'blk'), 'mp')
The draws below stay inside these ranges and needn't reach their ends.
All inputs are finite; a program needn't handle non-finite values.
Results may differ from the reference program's by a relative error of at most 0.005.
Values may be sent and summed in bfloat16 or wider, within the bound.
A program may use at most 128 MiB of HBM per device.

```python
import math
import jax
import jax.numpy as jnp
from jax import lax

D = 4096
HD = 256
HEADS = 8
SUMMARY = 256
TOKENS = 2048
DOCS = 8
FEATS = 2048
N_DP = 8


def shard_levels(stream_key, extent, pieces, smallest, largest):
    gain, own = 1.0, jax.random.fold_in(stream_key, 6)
    for position, shards_of in pieces:
        heights = jnp.exp(jax.random.uniform(jax.random.fold_in(own, position), (shards_of,), jnp.float32, smallest / len(pieces), largest / len(pieces)))
        gain = gain * jnp.repeat(heights, extent[position] // shards_of).reshape([-1 if axis == position else 1 for axis in range(len(extent))])
    return gain


def gaussian(key, extent, spread, limit, cuts=(), dtype=jnp.bfloat16):
    gain = shard_levels(key, extent, cuts, -0.22, 0.18) if cuts else 1.0
    entries = jax.random.normal(key, extent, jnp.float32) * spread * gain
    return jnp.minimum(jnp.maximum(entries, -limit), limit).astype(dtype)


def setup_inputs(seed: int = 0) -> dict:
    key_list = jax.random.split(jax.random.key(seed), 14)
    encoder_query = jnp.clip(jax.random.uniform(key_list[0], (DOCS, TOKENS, FEATS), jnp.float32, -0.4296875, 0.4296875) * shard_levels(key_list[0], (DOCS, TOKENS, FEATS), ((0, 8), (1, 8), (2, 4)), -0.4, 0.0), -0.4296875, 0.4296875).astype(jnp.bfloat16)
    encoder_keys = jnp.clip(jax.random.uniform(key_list[1], (DOCS, TOKENS, FEATS), jnp.float32, -0.4296875, 0.4296875) * shard_levels(key_list[1], (DOCS, TOKENS, FEATS), ((0, 8), (1, 8), (2, 4)), -0.4, 0.0), -0.4296875, 0.4296875).astype(jnp.bfloat16)
    encoder_values = gaussian(key_list[2], (DOCS, TOKENS, FEATS), 0.25, 1.5, ((0, 8), (1, 8), (2, 4)))
    encoder_output = gaussian(key_list[3], (DOCS, TOKENS, FEATS), 0.25, 1.5, ((0, 8), (1, 8), (2, 4)))
    encoder_cotangent = gaussian(key_list[4], (DOCS, TOKENS, FEATS), 16.0, 96.0, ((0, 8), (1, 8), (2, 4)))
    encoder_totals = jnp.clip(jnp.exp(math.log(4096.0) - 1.3862944 * jax.random.uniform(key_list[5], (DOCS, HEADS, TOKENS), jnp.float32) ** shard_levels(key_list[5], (DOCS, HEADS, TOKENS), ((0, 8), (1, 4), (2, 8)), -0.2, 0.2)), 1024.0, 4096.0)
    cross_keys = jnp.clip(jax.random.uniform(key_list[6], (DOCS, TOKENS, FEATS), jnp.float32, -0.4296875, 0.4296875) * shard_levels(key_list[6], (DOCS, TOKENS, FEATS), ((0, 8), (1, 8), (2, 4)), -0.4, 0.0), -0.4296875, 0.4296875).astype(jnp.bfloat16)
    cross_values = gaussian(key_list[7], (DOCS, TOKENS, FEATS), 0.25, 1.5, ((0, 8), (1, 8), (2, 4)))
    decoder_query = jnp.clip(jax.random.uniform(key_list[8], (DOCS, SUMMARY, FEATS), jnp.float32, -0.4296875, 0.4296875) * shard_levels(key_list[8], (DOCS, SUMMARY, FEATS), ((0, 8), (2, 4)), -0.4, 0.0), -0.4296875, 0.4296875).astype(jnp.bfloat16)
    decoder_output = gaussian(key_list[9], (DOCS, SUMMARY, FEATS), 0.25, 1.5, ((0, 8), (2, 4)))
    decoder_cotangent = gaussian(key_list[10], (DOCS, SUMMARY, FEATS), 32.0, 192.0, ((0, 8), (2, 4)))
    decoder_totals = jnp.clip(jnp.exp(math.log(4096.0) - 1.3862944 * jax.random.uniform(key_list[11], (DOCS, HEADS, SUMMARY), jnp.float32) ** shard_levels(key_list[11], (DOCS, HEADS, SUMMARY), ((0, 8), (1, 4)), -0.2, 0.2)), 1024.0, 4096.0)
    encoder_states = gaussian(key_list[12], (DOCS, TOKENS, D), (TOKENS * N_DP) ** -0.5, 0.046875, ((0, 8), (1, 8), (2, 4)))
    return {"encoder_query": encoder_query, "encoder_keys": encoder_keys, "encoder_values": encoder_values, "encoder_output": encoder_output, "encoder_cotangent": encoder_cotangent, "encoder_totals": encoder_totals, "cross_keys": cross_keys, "cross_values": cross_values, "decoder_query": decoder_query, "decoder_output": decoder_output, "decoder_cotangent": decoder_cotangent, "decoder_totals": decoder_totals, "encoder_states": encoder_states}


def head_grads(operands):
    head_query, head_keys, head_values, head_grad, head_totals, head_delta = operands
    scores = jnp.dot(head_query, head_keys.T, preferred_element_type=jnp.float32)
    softmax = jnp.exp(scores) / head_totals[:, None]
    weights = softmax.astype(jnp.bfloat16)
    value_grad = jnp.dot(weights.T, head_grad, preferred_element_type=jnp.float32)
    dprobs = jnp.dot(head_grad, head_values.T, preferred_element_type=jnp.float32)
    dscores = (softmax * (dprobs - head_delta[:, None])).astype(jnp.bfloat16)
    query_grad = jnp.dot(dscores, head_keys, preferred_element_type=jnp.float32)
    key_grad = jnp.dot(dscores.T, head_query, preferred_element_type=jnp.float32)
    return query_grad, key_grad, value_grad


def by_heads(array):
    return jnp.swapaxes(array.reshape(array.shape[0], HEADS, HD), 0, 1)


def from_heads(array):
    return jnp.swapaxes(array, 0, 1).reshape(array.shape[1], FEATS).astype(jnp.bfloat16)


def attention_grads(queries, key_rows, values, outputs, grad_out, totals):
    row_delta = jnp.sum(by_heads(grad_out).astype(jnp.float32) * by_heads(outputs).astype(jnp.float32), axis=-1)
    query_grad, key_grad, value_grad = lax.map(
        head_grads, (by_heads(queries), by_heads(key_rows), by_heads(values), by_heads(grad_out), totals, row_delta))
    return from_heads(query_grad), from_heads(key_grad), from_heads(value_grad)


def reference(encoder_query, encoder_keys, encoder_values, encoder_output, encoder_cotangent, encoder_totals,
              cross_keys, cross_values, decoder_query, decoder_output, decoder_cotangent, decoder_totals,
              encoder_states):
    enc_q, enc_k, enc_v, crs_k, crs_v, dec_q = [], [], [], [], [], []
    weight_grad = jnp.zeros((D, FEATS), jnp.float32)
    for document in range(DOCS):
        query_grad, key_grad, value_grad = attention_grads(
            encoder_query[document], encoder_keys[document], encoder_values[document],
            encoder_output[document], encoder_cotangent[document], encoder_totals[document])
        enc_q.append(query_grad)
        enc_k.append(key_grad)
        enc_v.append(value_grad)
        summary_grad, cross_kgrad, cross_vgrad = attention_grads(
            decoder_query[document], cross_keys[document], cross_values[document],
            decoder_output[document], decoder_cotangent[document], decoder_totals[document])
        dec_q.append(summary_grad)
        crs_k.append(cross_kgrad)
        crs_v.append(cross_vgrad)
        weight_grad = weight_grad + jnp.dot(encoder_states[document].T, cross_vgrad,
                                            preferred_element_type=jnp.float32)
    return (jnp.stack(enc_q), jnp.stack(enc_k), jnp.stack(enc_v), jnp.stack(crs_k), jnp.stack(crs_v),
            jnp.stack(dec_q), weight_grad)
```

```python
import jax
import jax.numpy as jnp
from jax import lax
from jax.experimental import pallas as pl
from jax.experimental.pallas import tpu as pltpu
from jax.sharding import PartitionSpec as P

HD = 256
NX = 4
NZ = 8
F32 = jnp.float32
BF16 = jnp.bfloat16
MESH = pl.DeviceIdType.MESH
ORDER = (0, 1, 3, 2)


def mm(a, b, ca, cb):
    return lax.dot_general(a, b, (((ca,), (cb,)), ((), ())), preferred_element_type=F32)


def row_sums(grad, out):
    product = grad.astype(F32) * out.astype(F32)
    high = product.astype(BF16)
    low = (product - high.astype(F32)).astype(BF16)
    ones = jnp.ones((8, HD), BF16)
    return mm(ones, high, 1, 1) + mm(ones, low, 1, 1)


def remote(src, dst, send, recv, device):
    return pltpu.make_async_remote_copy(
        src_ref=src, dst_ref=dst, send_sem=send, recv_sem=recv, device_id=device, device_id_type=MESH
    )


def arrived(dst, sem):
    pltpu.make_async_copy(dst, dst, sem).wait()


def push(src, dst, send, recv, device, here):
    @pl.when(here)
    def _():
        pltpu.make_async_copy(src, dst, recv).start()

    @pl.when(jnp.logical_not(here))
    def _():
        remote(src, dst, send, recv, device).start()


def pushed(src, dst, send, recv, device, here):
    @pl.when(jnp.logical_not(here))
    def _():
        remote(src, dst, send, recv, device).wait_send()


def kernel(
    eq, ek, ev, eo, ed, et, ck, cv, dq, do, dd, dt, es,
    out_q, out_k, out_v, out_ck, out_cv, out_dq, out_w,
    st_src, st_all, vg_all, z_src, z_recv, y_src, y_recv,
    kv, qd, stats_src, stats, acc, acc_recv, fin, dq_own, dq_send, dq_recv, dq_fin, raw,
    dec_src, dec_recv, dec_mine, dec_other, dec_all,
    st_s, st_r, sty_s, stc_s, vg_s, vg_r, z_s, z_r, y_s, y_r,
    kv_s, kv_r, kvc_s, qd_s, qd_r, qdy_s, sta_s, sta_r, stay_s,
    acc_s, acc_r, fin_s, raw_r, dqy_s, dqy_r, dqo_s,
    dec_s, dec_r, decy_s, decy_r, deca_s, deca_r,
):
    z = lax.axis_index("dp")
    blk = lax.axis_index("blk")
    mp = lax.axis_index("mp")
    yh, x = blk // NX, blk % NX
    yl, c = mp // 2, mp % 2
    oyh, oyl, oc = 1 - yh, 1 - yl, 1 - c

    def dev(z_=None, yh_=None, x_=None, yl_=None, c_=None):
        z_ = z if z_ is None else z_
        yh_ = yh if yh_ is None else yh_
        x_ = x if x_ is None else x_
        yl_ = yl if yl_ is None else yl_
        c_ = c if c_ is None else c_
        return (z_, yh_ * NX + x_, yl_ * 2 + c_)

    def at_x(d):
        return (x + d) % NX

    sibling = dev(c_=oc)
    ylo = dev(yl_=oyl)
    yhi = dev(yh_=oyh)

    barrier = pltpu.get_barrier_semaphore()
    partners = [dev(x_=at_x(d), c_=(c + dc) % 2) for d in range(NX) for dc in range(2) if d or dc]
    partners += [yhi, ylo]
    partners += [dev(z_=(z + d) % NZ) for d in range(1, NZ)]
    for partner in partners:
        pl.semaphore_signal(barrier, inc=1, device_id=partner, device_id_type=MESH)

    for k in range(4):
        piece = es[0, :, k * 256:(k + 1) * 256].T
        st_src[k] = piece.reshape(NX, 64, 256)
    st_all[mp, x] = st_src[:, x]

    for e in range(2):
        cols = slice(e * HD, (e + 1) * HD)
        keys, vals = ck[0, :, cols], cv[0, :, cols]
        query, grad = dq[0, :, cols], dd[0, :, cols]
        inv = 1.0 / dt[0, e:e + 1, :]
        delta = row_sums(grad, do[0, :, cols])[0:1, :]
        probs = jnp.exp(mm(keys, query, 1, 1)) * inv
        weights = probs.astype(BF16)
        dscores = (probs * (mm(vals, grad, 1, 1) - delta)).astype(BF16)
        value_grad = mm(weights, grad, 1, 0).astype(BF16)
        out_cv[0, :, cols] = value_grad
        vg_all[x, :, cols] = value_grad
        out_ck[0, :, cols] = mm(dscores, query, 1, 0).astype(BF16)
        part = mm(dscores, keys, 0, 0).astype(BF16)
        dec_src[:, :, cols] = part.reshape(NX, 64, HD)
        stats_src[e, 0:4, :] = jnp.broadcast_to(1.0 / et[0, e:e + 1, :], (4, 256))
        stats_src[e, 4:8, :] = row_sums(ed[0, :, cols], eo[0, :, cols])[0:4, :]
    dec_recv[x] = dec_src[x]

    pl.semaphore_wait(barrier, len(partners))

    st_out = [remote(st_src.at[:, at_x(d)], st_all.at[mp, x], st_s.at[d], st_r.at[mp, x], dev(x_=at_x(d)))
              for d in (1, 3, 2)]
    vg_out = [remote(vg_all.at[x], vg_all.at[x], vg_s.at[d], vg_r.at[x], dev(x_=at_x(d))) for d in (1, 3, 2)]
    dec_out = [remote(dec_src.at[at_x(d)], dec_recv.at[x], dec_s.at[d], dec_r.at[x], dev(x_=at_x(d)))
               for d in (1, 3, 2)]
    for cp in st_out:
        cp.start()

    def st_to_ylo(s):
        return remote(st_all.at[mp, s], st_all.at[mp, s], sty_s.at[s], st_r.at[mp, s], ylo)

    def st_to_sibling(m, k, s):
        return remote(st_all.at[m, s], st_all.at[m, s], stc_s.at[k, s], st_r.at[m, s], sibling)

    mine, other = mp, oyl * 2 + c
    st_to_ylo(x).start()
    st_to_sibling(mine, 0, x).start()
    for cp in vg_out:
        cp.start()

    enc_out = []
    for i in range(2):
        e = (x + i) % 2
        xt = 2 * c + e
        cols = pl.ds(pl.multiple_of(e * HD, HD), HD)
        for a, src in ((0, ek), (1, ev)):
            enc_out.append((src.at[0, :, cols], kv.at[a, x], kv_s.at[i, a], kv_r.at[a, x],
                            dev(x_=xt, c_=a), jnp.logical_and(xt == x, c == a)))
        here = jnp.logical_and(xt == x, c == yh)
        target = dev(x_=xt, c_=yh)
        for a, src in ((0, eq), (1, ed)):
            enc_out.append((src.at[0, :, cols], qd.at[x, a], qd_s.at[i, a], qd_r.at[x, a], target, here))
        enc_out.append((stats_src.at[e], stats.at[x], sta_s.at[i], sta_r.at[x], target, here))
    for args in enc_out:
        push(*args)
    for cp in dec_out:
        cp.start()

    for d in (1, 3, 2):
        s = at_x(d)
        arrived(st_all.at[mine, s], st_r.at[mine, s])
        st_to_ylo(s).start()
        st_to_sibling(mine, 0, s).start()
    for d in ORDER:
        s = at_x(d)
        arrived(st_all.at[other, s], st_r.at[other, s])
        st_to_sibling(other, 1, s).start()

    for d in (1, 3, 2):
        s = at_x(d)
        arrived(dec_recv.at[s], dec_r.at[s])
    total = dec_recv[0].astype(F32)
    for s in range(1, NX):
        total = total + dec_recv[s].astype(F32)
    dec_mine[...] = total
    dec_swap = remote(dec_mine, dec_other, decy_s, decy_r, yhi)
    dec_swap.start()

    def kv_to_sibling(s):
        return remote(kv.at[c, s], kv.at[c, s], kvc_s.at[s], kv_r.at[c, s], sibling)

    def qd_to_yhi(s):
        return [remote(qd.at[s, a], qd.at[s, a], qdy_s.at[s, a], qd_r.at[s, a], yhi) for a in range(2)] + [
            remote(stats.at[s], stats.at[s], stay_s.at[s], sta_r.at[s], yhi)]

    def qd_arrived(s):
        for a in range(2):
            arrived(qd.at[s, a], qd_r.at[s, a])
        arrived(stats.at[s], sta_r.at[s])

    first_hand = c == yh
    for d in ORDER:
        s = at_x(d)
        arrived(kv.at[c, s], kv_r.at[c, s])
        kv_to_sibling(s).start()

        @pl.when(first_hand)
        def _(s=s):
            qd_arrived(s)
            for cp in qd_to_yhi(s):
                cp.start()

    for d in (1, 3, 2):
        s = at_x(d)
        arrived(vg_all.at[s], vg_r.at[s])
    for s in range(NX):
        arrived(st_all.at[yl * 2 + oc, s], st_r.at[yl * 2 + oc, s])
        arrived(st_all.at[oyl * 2 + oc, s], st_r.at[oyl * 2 + oc, s])

    z_out = []
    for k in range(4):
        m = (z // 2 + k) % 4
        part = mm(st_all[m, 0].reshape(256, 256), vg_all[0], 1, 0)
        for s in range(1, NX):
            part = part + mm(st_all[m, s].reshape(256, 256), vg_all[s], 1, 0)
        z_src[k] = part.astype(BF16).reshape(2, 128, 512)
        for l in range(2):
            zt = 2 * m + l
            args = (z_src.at[k, l], z_recv.at[z], z_s.at[k, l], z_r.at[z], dev(z_=zt), zt == z)
            push(*args)
            z_out.append(args)

    dec_swap.wait()
    dec_all[x] = (dec_mine[...] + dec_other[...]).astype(BF16)
    deca_out = [remote(dec_all.at[x], dec_all.at[x], deca_s.at[d], deca_r.at[x], dev(x_=at_x(d))) for d in (1, 3, 2)]
    for cp in deca_out:
        cp.start()

    for s in range(NX):
        arrived(kv.at[oc, s], kv_r.at[oc, s])

    def dq_to_yhi(s):
        return remote(dq_send.at[s], dq_recv.at[s], dqy_s.at[s], dqy_r.at[s], yhi)

    def acc_to_sibling(b):
        return remote(acc.at[oc, b], acc_recv.at[b], acc_s.at[b], acc_r.at[b], sibling)

    for i, d in enumerate(ORDER):
        s = at_x(d)

        @pl.when(jnp.logical_not(first_hand))
        def _(s=s):
            qd_arrived(s)

        query, grad = qd[s, 0], qd[s, 1]
        inv, delta = stats[s, 0:1, :], stats[s, 4:5, :]
        grad_q = jnp.zeros((256, HD), F32)
        for h in range(2):
            keys = kv[0, 2 * h:2 * h + 2].reshape(512, HD)
            vals = kv[1, 2 * h:2 * h + 2].reshape(512, HD)
            probs = jnp.exp(mm(keys, query, 1, 1)) * inv
            weights = probs.astype(BF16)
            dscores = (probs * (mm(vals, grad, 1, 1) - delta)).astype(BF16)
            value_part = mm(weights, grad, 1, 0).reshape(2, 256, HD)
            key_part = mm(dscores, query, 1, 0).reshape(2, 256, HD)
            grad_q = grad_q + mm(dscores, keys, 0, 0)
            if i:
                key_part = key_part + acc[0, 2 * h:2 * h + 2]
                value_part = value_part + acc[1, 2 * h:2 * h + 2]
            acc[0, 2 * h:2 * h + 2] = key_part
            acc[1, 2 * h:2 * h + 2] = value_part
            if i == NX - 1:
                for b in (2 * h, 2 * h + 1):
                    acc_to_sibling(b).start()

        @pl.when(first_hand)
        def _(s=s, grad_q=grad_q):
            dq_own[s] = grad_q

        @pl.when(jnp.logical_not(first_hand))
        def _(s=s, grad_q=grad_q):
            dq_send[s] = grad_q.astype(BF16)
            dq_to_yhi(s).start()

    e_of = x % 2
    owner_c = x // 2
    fin_out = []
    for b in range(NX):
        arrived(acc_recv.at[b], acc_r.at[b])
        fin[b] = (acc[c, b] + acc_recv[b]).astype(BF16)
        args = (fin.at[b], raw.at[c, e_of], fin_s.at[b], raw_r.at[c, e_of], dev(x_=b, c_=owner_c),
                jnp.logical_and(b == x, c == owner_c))
        push(*args)
        fin_out.append(args)

    def dq_args(s):
        return (dq_fin.at[s], raw.at[2, e_of], dqo_s.at[s], raw_r.at[2, e_of], dev(x_=s, c_=owner_c),
                jnp.logical_and(s == x, c == owner_c))

    @pl.when(first_hand)
    def _():
        for d in ORDER:
            s = at_x(d)
            arrived(dq_recv.at[s], dqy_r.at[s])
            dq_fin[s] = (dq_own[s] + dq_recv[s].astype(F32)).astype(BF16)
            push(*dq_args(s))

    for s in range(NZ):
        arrived(z_recv.at[s], z_r.at[s])
    w = z_recv[0].astype(F32)
    for s in range(1, NZ):
        w = w + z_recv[s].astype(F32)
    y_src[...] = w.reshape(2, 64, 512)
    y_swap = remote(y_src.at[oyh], y_recv, y_s, y_r, yhi)
    y_swap.start()

    for d in (1, 3, 2):
        s = at_x(d)
        arrived(dec_all.at[s], deca_r.at[s])
    out_dq[0] = dec_all[...].reshape(256, 512)

    for e in range(2):
        cols = slice(e * HD, (e + 1) * HD)
        for a, out in ((0, out_k), (1, out_v), (2, out_q)):
            arrived(raw.at[a, e], raw_r.at[a, e])
            out[0, :, cols] = raw[a, e]

    y_swap.wait()
    out_w[...] = y_src[yh] + y_recv[...]

    for cp in st_out + vg_out + dec_out + deca_out:
        cp.wait_send()
    for d in range(NX):
        st_to_ylo(d).wait_send()
        st_to_sibling(mine, 0, d).wait_send()
        st_to_sibling(other, 1, d).wait_send()
        kv_to_sibling(d).wait_send()
        acc_to_sibling(d).wait_send()
    for args in enc_out + z_out + fin_out:
        pushed(*args)

    @pl.when(first_hand)
    def _():
        for s in range(NX):
            for cp in qd_to_yhi(s):
                cp.wait_send()
            pushed(*dq_args(s))

    @pl.when(jnp.logical_not(first_hand))
    def _():
        for s in range(NX):
            dq_to_yhi(s).wait_send()


def body(*arrays):
    vmem = pl.BlockSpec(memory_space=pltpu.VMEM)
    dma = pltpu.SemaphoreType.DMA
    outs = [jax.ShapeDtypeStruct((1, 256, 512), BF16) for _ in range(6)]
    outs.append(jax.ShapeDtypeStruct((64, 512), F32))
    buffers = [
        ((4, NX, 64, 256), BF16), ((4, NX, 4, 64, 256), BF16), ((NX, 256, 512), BF16),
        ((4, 2, 128, 512), BF16), ((NZ, 128, 512), BF16), ((2, 64, 512), F32), ((64, 512), F32),
        ((2, NX, 256, HD), BF16), ((NX, 2, 256, HD), BF16), ((2, 8, 256), F32), ((NX, 8, 256), F32),
        ((2, NX, 256, HD), F32), ((NX, 256, HD), F32), ((NX, 256, HD), BF16), ((NX, 256, HD), F32),
        ((NX, 256, HD), BF16), ((NX, 256, HD), BF16), ((NX, 256, HD), BF16), ((3, 2, 256, HD), BF16),
        ((NX, 64, 512), BF16), ((NX, 64, 512), BF16), ((64, 512), F32), ((64, 512), F32), ((NX, 64, 512), BF16),
    ]
    semaphores = [
        (NX,), (4, NX), (NX,), (2, NX), (NX,), (NX,), (4, 2), (NZ,), None, None,
        (2, 2), (2, NX), (NX,), (2, 2), (NX, 2), (NX, 2), (2,), (NX,), (NX,),
        (NX,), (NX,), (NX,), (3, 2), (NX,), (NX,), (NX,),
        (NX,), (NX,), None, None, (NX,), (NX,),
    ]
    scratch = [pltpu.VMEM(shape, dtype) for shape, dtype in buffers]
    scratch += [dma if shape is None else dma(shape) for shape in semaphores]
    return tuple(pl.pallas_call(
        kernel,
        out_shape=outs,
        in_specs=[vmem] * 13,
        out_specs=[vmem] * 7,
        scratch_shapes=scratch,
        compiler_params=pltpu.CompilerParams(
            collective_id=0, has_side_effects=True, vmem_limit_bytes=48 * 1024 * 1024
        ),
        cost_estimate=pl.CostEstimate(flops=5_000_000_000, bytes_accessed=6_000_000, transcendentals=1_200_000),
        name="grads",
    )(*arrays))


def solution(mesh):
    rows = P("dp", "blk", "mp")
    tokens = P("dp", None, "mp")
    in_specs = (rows, rows, rows, rows, rows, P("dp", "mp", "blk"), rows, rows, tokens, tokens, tokens,
                P("dp", "mp", None), rows)
    out_specs = (rows, rows, rows, rows, rows, tokens, P(("dp", "blk"), "mp"))
    return jax.shard_map(body, mesh=mesh, in_specs=in_specs, out_specs=out_specs, check_vma=False)
```

```python
import jax
import jax.numpy as jnp
from jax import lax
from jax.experimental import pallas as pl
from jax.experimental.pallas import tpu as pltpu
from jax.sharding import PartitionSpec as P

HD = 256
NX = 4
NZ = 8
F32 = jnp.float32
BF16 = jnp.bfloat16
MESH = pl.DeviceIdType.MESH
ORDER = (0, 1, 3, 2)
RELAY = False
GATE = 0
SWAP = F32
PLAN = 1


def mm(a, b, ca, cb):
    return lax.dot_general(a, b, (((ca,), (cb,)), ((), ())), preferred_element_type=F32)


def row_sums(grad, out):
    product = grad.astype(F32) * out.astype(F32)
    high = product.astype(BF16)
    low = (product - high.astype(F32)).astype(BF16)
    ones = jnp.ones((8, HD), BF16)
    return mm(ones, high, 1, 1) + mm(ones, low, 1, 1)


def remote(src, dst, send, recv, device):
    return pltpu.make_async_remote_copy(
        src_ref=src, dst_ref=dst, send_sem=send, recv_sem=recv, device_id=device, device_id_type=MESH
    )


def arrived(dst, sem):
    pltpu.make_async_copy(dst, dst, sem).wait()


def push(src, dst, send, recv, device, here):
    @pl.when(here)
    def _():
        pltpu.make_async_copy(src, dst, recv).start()

    @pl.when(jnp.logical_not(here))
    def _():
        remote(src, dst, send, recv, device).start()


def pushed(src, dst, send, recv, device, here):
    @pl.when(jnp.logical_not(here))
    def _():
        remote(src, dst, send, recv, device).wait_send()


def kernel(
    eq, ek, ev, eo, ed, et, ck, cv, dq, do, dd, dt, es,
    raw, out_ck, out_cv, out_dq, out_w,
    es_v, ck_v, cv_v, dq_v, do_v, dd_v, dt_v, eo_v, ed_v, et_v, load_s,
    st_src, st_all, vg_all, z_src, z_recv, y_own, y_src, y_recv,
    kv, qd, stats_src, stats, acc, acc_recv, fin, dq_own, dq_send, dq_recv, dq_fin,
    dec_src, dec_recv, dec_mine, dec_other, dec_all,
    st_s, st_r, sty_s, stc_s, vg_s, vg_r, z_s, z_r, y_s, y_r,
    kv_s, kv_r, kvc_s, qd_s, qd_r, qdy_s, sta_s, sta_r, stay_s,
    acc_s, acc_r, fin_s, raw_r, dqy_s, dqy_r, dqo_s,
    dec_s, dec_r, decy_s, decy_r, deca_s, deca_r,
):
    z = lax.axis_index("dp")
    blk = lax.axis_index("blk")
    mp = lax.axis_index("mp")
    yh, x = blk // NX, blk % NX
    yl, c = mp // 2, mp % 2
    oyh, oyl, oc = 1 - yh, 1 - yl, 1 - c

    def dev(z_=None, yh_=None, x_=None, yl_=None, c_=None):
        z_ = z if z_ is None else z_
        yh_ = yh if yh_ is None else yh_
        x_ = x if x_ is None else x_
        yl_ = yl if yl_ is None else yl_
        c_ = c if c_ is None else c_
        return (z_, yh_ * NX + x_, yl_ * 2 + c_)

    def at_x(d):
        return (x + d) % NX

    sibling = dev(c_=oc)
    ylo = dev(yl_=oyl)
    yhi = dev(yh_=oyh)

    barrier = pltpu.get_barrier_semaphore()
    partners = [dev(x_=at_x(d), c_=(c + dc) % 2) for d in range(NX) for dc in range(2) if d or dc]
    partners += [yhi, ylo]
    partners += [dev(z_=(z + d) % NZ) for d in range(1, NZ)]
    for partner in partners:
        pl.semaphore_signal(barrier, inc=1, device_id=partner, device_id_type=MESH)

    loads = [pltpu.make_async_copy(src, dst, load_s.at[i]) for i, (src, dst) in enumerate(
        ((es, es_v), (ck, ck_v), (dq, dq_v), (dt, dt_v), (dd, dd_v), (cv, cv_v), (do, do_v),
         (eo, eo_v), (ed, ed_v), (et, et_v)))]
    for cp in loads:
        cp.start()

    loads[0].wait()
    for k in range(4):
        piece = es_v[0, :, k * 256:(k + 1) * 256].T
        st_src[k] = piece.reshape(NX, 64, 256)
    st_all[mp, x] = st_src[:, x]

    pl.semaphore_wait(barrier, len(partners))

    st_out = [remote(st_src.at[:, at_x(d)], st_all.at[mp, x], st_s.at[d], st_r.at[mp, x], dev(x_=at_x(d)))
              for d in (1, 3, 2)]

    def vg_to(e, s, d):
        return remote(vg_all.at[e, s], vg_all.at[e, s], vg_s.at[e, d], vg_r.at[e, s], dev(x_=at_x(d)))

    dec_out = [remote(dec_src.at[at_x(d)], dec_recv.at[x], dec_s.at[d], dec_r.at[x], dev(x_=at_x(d)))
               for d in (1, 3, 2)]
    for cp in st_out:
        cp.start()

    def st_to_ylo(s):
        return remote(st_all.at[mp, s], st_all.at[mp, s], sty_s.at[s], st_r.at[mp, s], ylo)

    def st_to_sibling(m, k, s):
        return remote(st_all.at[m, s], st_all.at[m, s], stc_s.at[k, s], st_r.at[m, s], sibling)

    mine, other = mp, oyl * 2 + c
    st_to_ylo(x).start()
    st_to_sibling(mine, 0, x).start()

    enc_out, st_out_args = [], []
    for i in range(2):
        e = (x + i) % 2
        xt = 2 * c + e
        cols = pl.ds(pl.multiple_of(e * HD, HD), HD)
        for a, src in ((0, ek), (1, ev)):
            enc_out.append((src.at[0, :, cols], kv.at[a, x], kv_s.at[i, a], kv_r.at[a, x],
                            dev(x_=xt, c_=a), jnp.logical_and(xt == x, c == a), 0))
        here = jnp.logical_and(xt == x, c == yh)
        target = dev(x_=xt, c_=yh)
        for a, src in ((0, eq), (1, ed)):
            enc_out.append((src.at[0, :, cols], qd.at[x, a], qd_s.at[i, a], qd_r.at[x, a], target, here, 1))
        st_out_args.append((stats_src.at[e], stats.at[x], sta_s.at[i], sta_r.at[x], target, here))

    qd_out, kv_out = [args for args in enc_out if args[6]], [args for args in enc_out if not args[6]]
    qd_out, kv_out = [args[:6] for args in qd_out], [args[:6] for args in kv_out]

    def send(some):
        for args in some:
            push(*args)

    cross = []

    def cross_values(e):
        cols = slice(e * HD, (e + 1) * HD)
        probs = jnp.exp(mm(ck_v[0, :, cols], dq_v[0, :, cols], 1, 1)) * (1.0 / dt_v[0, e:e + 1, :])
        value_grad = mm(probs.astype(BF16), dd_v[0, :, cols], 1, 0).astype(BF16)
        out_cv[0, :, cols] = value_grad
        vg_all[e, x] = value_grad
        cross.append(probs)

    def send_values(e):
        for d in (1, 3):
            vg_to(e, x, d).start()
        if not RELAY:
            vg_to(e, x, 2).start()

    def send_stats():
        for cp in loads[7:]:
            cp.wait()
        for e in range(2):
            cols = slice(e * HD, (e + 1) * HD)
            stats_src[e, 0:4, :] = jnp.broadcast_to(1.0 / et_v[0, e:e + 1, :], (4, 256))
            stats_src[e, 4:8, :] = row_sums(ed_v[0, :, cols], eo_v[0, :, cols])[0:4, :]
        send(st_out_args)

    def cross_rest():
        for e in range(2):
            cols = slice(e * HD, (e + 1) * HD)
            keys, query, grad = ck_v[0, :, cols], dq_v[0, :, cols], dd_v[0, :, cols]
            delta = row_sums(grad, do_v[0, :, cols])[0:1, :]
            dscores = (cross[e] * (mm(cv_v[0, :, cols], grad, 1, 1) - delta)).astype(BF16)
            out_ck[0, :, cols] = mm(dscores, query, 1, 0).astype(BF16)
            dec_src[:, :, cols] = mm(dscores, keys, 0, 0).astype(BF16).reshape(NX, 64, HD)
        dec_recv[x] = dec_src[x]
        for cp in dec_out:
            cp.start()

    def states_first():
        for d in (1, 3, 2):
            s = at_x(d)
            arrived(st_all.at[mine, s], st_r.at[mine, s])
            st_to_ylo(s).start()
            st_to_sibling(mine, 0, s).start()

    def states_second():
        for d in ORDER:
            s = at_x(d)
            arrived(st_all.at[other, s], st_r.at[other, s])
            st_to_sibling(other, 1, s).start()

    def states_third():
        for s in range(NX):
            arrived(st_all.at[yl * 2 + oc, s], st_r.at[yl * 2 + oc, s])
            arrived(st_all.at[oyl * 2 + oc, s], st_r.at[oyl * 2 + oc, s])

    def relay(e):
        return 1 + 2 * ((c + e) % 2)

    def vg_relayed(e):
        d = relay(e)
        return remote(vg_all.at[e, (x + NX - d) % NX], vg_all.at[e, (x + NX - d) % NX], vg_s.at[e, 2],
                      vg_r.at[e, (x + NX - d) % NX], dev(x_=at_x(d)))

    def values_arrive(e):
        if RELAY:
            d = relay(e)
            first = (x + NX - d) % NX
            arrived(vg_all.at[e, first], vg_r.at[e, first])
            vg_relayed(e).start()
            arrived(vg_all.at[e, (x + d) % NX], vg_r.at[e, (x + d) % NX])
            arrived(vg_all.at[e, at_x(2)], vg_r.at[e, at_x(2)])
        else:
            for d in (1, 3, 2):
                arrived(vg_all.at[e, at_x(d)], vg_r.at[e, at_x(d)])

    def kv_to_sibling(s):
        return remote(kv.at[c, s], kv.at[c, s], kvc_s.at[s], kv_r.at[c, s], sibling)

    def qd_to_yhi(s):
        return [remote(qd.at[s, a], qd.at[s, a], qdy_s.at[s, a], qd_r.at[s, a], yhi) for a in range(2)] + [
            remote(stats.at[s], stats.at[s], stay_s.at[s], sta_r.at[s], yhi)]

    def qd_arrived(s):
        for a in range(2):
            arrived(qd.at[s, a], qd_r.at[s, a])
        arrived(stats.at[s], sta_r.at[s])

    first_hand = c == yh

    dec_swap = remote(dec_mine, dec_other, decy_s, decy_r, yhi)
    z_out = []

    def decoder_sum():
        for d in (1, 3, 2):
            s = at_x(d)
            arrived(dec_recv.at[s], dec_r.at[s])
        total = dec_recv[0].astype(F32)
        for s in range(1, NX):
            total = total + dec_recv[s].astype(F32)
        dec_mine[...] = total
        dec_swap.start()

    def queries_forward():
        for d in ORDER:
            s = at_x(d)

            @pl.when(first_hand)
            def _(s=s):
                qd_arrived(s)
                for cp in qd_to_yhi(s):
                    cp.start()

    def keys_forward():
        for d in ORDER:
            s = at_x(d)
            arrived(kv.at[c, s], kv_r.at[c, s])
            kv_to_sibling(s).start()

    def weight_gradient(e):
        for k in range(4):
            m = (z // 2 + k) % 4
            part = mm(st_all[m, 0].reshape(256, 256), vg_all[e, 0], 1, 0)
            for s in range(1, NX):
                part = part + mm(st_all[m, s].reshape(256, 256), vg_all[e, s], 1, 0)
            z_src[e, k] = part.astype(BF16).reshape(2, 128, HD)
            for l in range(2):
                zt = 2 * m + l
                args = (z_src.at[e, k, l], z_recv.at[e, z], z_s.at[e, k, l], z_r.at[e, z], dev(z_=zt), zt == z)
                push(*args)
                z_out.append(args)

    for cp in loads[1:7]:
        cp.wait()
    if PLAN == 0:
        cross_values(0)
        send_values(0)
        send(qd_out)
        cross_values(1)
        send_values(1)
        send(kv_out)
        send_stats()
        cross_rest()
        states_first()
        states_second()
        values_arrive(0)
        states_third()
        weight_gradient(0)
        queries_forward()
        values_arrive(1)
        weight_gradient(1)
        keys_forward()
        decoder_sum()
    elif PLAN == 1:
        cross_values(0)
        send_values(0)
        cross_values(1)
        send_stats()
        states_first()
        send(qd_out)
        states_second()
        values_arrive(0)
        send_values(1)
        states_third()
        weight_gradient(0)
        queries_forward()
        send(kv_out)
        values_arrive(1)
        weight_gradient(1)
        cross_rest()
        keys_forward()
        decoder_sum()
    elif PLAN == 2:
        send(qd_out)
        cross_values(0)
        send_values(0)
        cross_values(1)
        send_values(1)
        send(kv_out)
        send_stats()
        cross_rest()
        states_first()
        queries_forward()
        states_second()
        values_arrive(0)
        states_third()
        weight_gradient(0)
        values_arrive(1)
        weight_gradient(1)
        keys_forward()
        decoder_sum()

    dec_swap.wait()
    dec_all[x] = (dec_mine[...] + dec_other[...]).astype(BF16)
    deca_out = [remote(dec_all.at[x], dec_all.at[x], deca_s.at[d], deca_r.at[x], dev(x_=at_x(d))) for d in (1, 3, 2)]
    for cp in deca_out:
        cp.start()

    for s in range(NX):
        arrived(kv.at[oc, s], kv_r.at[oc, s])

    def dq_to_yhi(s):
        return remote(dq_send.at[s], dq_recv.at[s], dqy_s.at[s], dqy_r.at[s], yhi)

    def acc_to_sibling(b):
        return remote(acc.at[oc, b], acc_recv.at[b], acc_s.at[b], acc_r.at[b], sibling)

    for i, d in enumerate(ORDER):
        s = at_x(d)

        @pl.when(jnp.logical_not(first_hand))
        def _(s=s):
            qd_arrived(s)

        query, grad = qd[s, 0], qd[s, 1]
        inv, delta = stats[s, 0:1, :], stats[s, 4:5, :]
        grad_q = jnp.zeros((256, HD), F32)
        for h in range(2):
            keys = kv[0, 2 * h:2 * h + 2].reshape(512, HD)
            vals = kv[1, 2 * h:2 * h + 2].reshape(512, HD)
            probs = jnp.exp(mm(keys, query, 1, 1)) * inv
            weights = probs.astype(BF16)
            dscores = (probs * (mm(vals, grad, 1, 1) - delta)).astype(BF16)
            value_part = mm(weights, grad, 1, 0).reshape(2, 256, HD)
            key_part = mm(dscores, query, 1, 0).reshape(2, 256, HD)
            grad_q = grad_q + mm(dscores, keys, 0, 0)
            if i:
                key_part = key_part + acc[0, 2 * h:2 * h + 2]
                value_part = value_part + acc[1, 2 * h:2 * h + 2]
            acc[0, 2 * h:2 * h + 2] = key_part
            acc[1, 2 * h:2 * h + 2] = value_part
            if i == NX - 1:
                for b in (2 * h, 2 * h + 1):
                    acc_to_sibling(b).start()

        @pl.when(first_hand)
        def _(s=s, grad_q=grad_q):
            dq_own[s] = grad_q

        @pl.when(jnp.logical_not(first_hand))
        def _(s=s, grad_q=grad_q):
            dq_send[s] = grad_q.astype(BF16)
            dq_to_yhi(s).start()

    e_of = x % 2
    owner_c = x // 2
    fin_out = []
    for b in range(NX):
        arrived(acc_recv.at[b], acc_r.at[b])
        fin[b] = (acc[c, b] + acc_recv[b]).astype(BF16)
        args = (fin.at[b], raw.at[c, e_of], fin_s.at[b], raw_r.at[c, e_of], dev(x_=b, c_=owner_c),
                jnp.logical_and(b == x, c == owner_c))
        push(*args)
        fin_out.append(args)

    def dq_args(s):
        return (dq_fin.at[s], raw.at[2, e_of], dqo_s.at[s], raw_r.at[2, e_of], dev(x_=s, c_=owner_c),
                jnp.logical_and(s == x, c == owner_c))

    @pl.when(first_hand)
    def _():
        for d in ORDER:
            s = at_x(d)
            arrived(dq_recv.at[s], dqy_r.at[s])
            dq_fin[s] = (dq_own[s] + dq_recv[s].astype(F32)).astype(BF16)
            push(*dq_args(s))

    def y_swap(e):
        return remote(y_src.at[e, oyh], y_recv.at[e], y_s.at[e], y_r.at[e], yhi)

    for e in range(2):
        for s in range(NZ):
            arrived(z_recv.at[e, s], z_r.at[e, s])
        w = z_recv[e, 0].astype(F32)
        for s in range(1, NZ):
            w = w + z_recv[e, s].astype(F32)
        w = w.reshape(2, 64, HD)
        y_own[e] = w
        y_src[e] = w.astype(y_src.dtype)
        y_swap(e).start()

    for d in (1, 3, 2):
        s = at_x(d)
        arrived(dec_all.at[s], deca_r.at[s])
    out_dq[0] = dec_all[...].reshape(256, 512)

    for e in range(2):
        for a in range(3):
            arrived(raw.at[a, e], raw_r.at[a, e])

    for e in range(2):
        y_swap(e).wait()
        out_w[:, e * HD:(e + 1) * HD] = y_own[e, yh] + y_recv[e].astype(F32)

    for cp in st_out + dec_out + deca_out + ([vg_relayed(e) for e in range(2)] if RELAY else []):
        cp.wait_send()
    for d in range(NX):
        st_to_ylo(d).wait_send()
        st_to_sibling(mine, 0, d).wait_send()
        st_to_sibling(other, 1, d).wait_send()
        kv_to_sibling(d).wait_send()
        acc_to_sibling(d).wait_send()
    for e in range(2):
        for d in (1, 3) if RELAY else (1, 3, 2):
            vg_to(e, x, d).wait_send()
    for args in qd_out + kv_out + st_out_args + z_out + fin_out:
        pushed(*args)

    @pl.when(first_hand)
    def _():
        for s in range(NX):
            for cp in qd_to_yhi(s):
                cp.wait_send()
            pushed(*dq_args(s))

    @pl.when(jnp.logical_not(first_hand))
    def _():
        for s in range(NX):
            dq_to_yhi(s).wait_send()


def finish(raw, in_ck, in_cv, in_dq, in_w, out_q, out_k, out_v, out_ck, out_cv, out_dq, out_w, sems):
    copies = []
    for a, out in ((0, out_k), (1, out_v), (2, out_q)):
        for e in range(2):
            copies.append((raw.at[a, e], out.at[0, :, e * HD:(e + 1) * HD]))
    copies += [(in_ck, out_ck), (in_cv, out_cv), (in_dq, out_dq), (in_w, out_w)]
    copies = [pltpu.make_async_copy(src, dst, sems.at[i]) for i, (src, dst) in enumerate(copies)]
    for cp in copies:
        cp.start()
    for cp in copies:
        cp.wait()


def body(*arrays):
    hbm = pl.BlockSpec(memory_space=pltpu.HBM)
    vmem = pl.BlockSpec(memory_space=pltpu.VMEM)
    dma = pltpu.SemaphoreType.DMA
    grads = [((1, 256, 512), BF16)] * 3 + [((64, 512), F32)]
    outs = [pltpu.VMEM((3, 2, 256, HD), BF16)] + [pltpu.VMEM(shape, dtype) for shape, dtype in grads]
    buffers = [((1, 256, 1024), BF16)] + [((1, 256, 512), BF16)] * 5 + [((1, 2, 256), F32)]
    buffers += [((1, 256, 512), BF16)] * 2 + [((1, 2, 256), F32)]
    scratch = [pltpu.VMEM(shape, dtype) for shape, dtype in buffers] + [dma((10,))]
    buffers = [
        ((4, NX, 64, 256), BF16), ((4, NX, 4, 64, 256), BF16), ((2, NX, 256, HD), BF16),
        ((2, 4, 2, 128, HD), BF16), ((2, NZ, 128, HD), BF16), ((2, 2, 64, HD), F32), ((2, 2, 64, HD), SWAP),
        ((2, 64, HD), SWAP),
        ((2, NX, 256, HD), BF16), ((NX, 2, 256, HD), BF16), ((2, 8, 256), F32), ((NX, 8, 256), F32),
        ((2, NX, 256, HD), F32), ((NX, 256, HD), F32), ((NX, 256, HD), BF16), ((NX, 256, HD), F32),
        ((NX, 256, HD), BF16), ((NX, 256, HD), BF16), ((NX, 256, HD), BF16),
        ((NX, 64, 512), BF16), ((NX, 64, 512), BF16), ((64, 512), F32), ((64, 512), F32), ((NX, 64, 512), BF16),
    ]
    semaphores = [
        (NX,), (4, NX), (NX,), (2, NX), (2, NX), (2, NX), (2, 4, 2), (2, NZ), (2,), (2,),
        (2, 2), (2, NX), (NX,), (2, 2), (NX, 2), (NX, 2), (2,), (NX,), (NX,),
        (NX,), (NX,), (NX,), (3, 2), (NX,), (NX,), (NX,),
        (NX,), (NX,), None, None, (NX,), (NX,),
    ]
    scratch += [pltpu.VMEM(shape, dtype) for shape, dtype in buffers]
    scratch += [dma if shape is None else dma(shape) for shape in semaphores]
    parts = pl.pallas_call(
        kernel,
        out_shape=outs,
        in_specs=[hbm] * 13,
        out_specs=[vmem] * 5,
        scratch_shapes=scratch,
        compiler_params=pltpu.CompilerParams(
            collective_id=0, has_side_effects=True, vmem_limit_bytes=40 * 1024 * 1024
        ),
        cost_estimate=pl.CostEstimate(flops=5_000_000_000, bytes_accessed=6_000_000, transcendentals=1_200_000),
        name="grads",
    )(*[pltpu.with_memory_space_constraint(array, pltpu.HBM) for array in arrays])
    shapes = [jax.ShapeDtypeStruct(shape, dtype) for shape, dtype in [((1, 256, 512), BF16)] * 3 + grads]
    return tuple(pl.pallas_call(
        finish,
        out_shape=shapes,
        in_specs=[vmem] * 5,
        out_specs=[hbm] * 7,
        scratch_shapes=[dma((10,))],
        compiler_params=pltpu.CompilerParams(vmem_limit_bytes=2 * 1024 * 1024),
        name="finish",
    )(*[pltpu.with_memory_space_constraint(part, pltpu.VMEM) for part in parts]))


def solution(mesh):
    rows = P("dp", "blk", "mp")
    tokens = P("dp", None, "mp")
    in_specs = (rows, rows, rows, rows, rows, P("dp", "mp", "blk"), rows, rows, tokens, tokens, tokens,
                P("dp", "mp", None), rows)
    out_specs = (rows, rows, rows, rows, rows, tokens, P(("dp", "blk"), "mp"))
    return jax.shard_map(body, mesh=mesh, in_specs=in_specs, out_specs=out_specs, check_vma=False)
```

```python
import jax
import jax.numpy as jnp
from jax import lax
from jax.experimental import pallas as pl
from jax.experimental.pallas import tpu as pltpu
from jax.sharding import PartitionSpec as P

HD = 256
NX = 4
NZ = 8
F32 = jnp.float32
BF16 = jnp.bfloat16
MESH = pl.DeviceIdType.MESH
ORDER = (0, 1, 3, 2)
SWAP = F32


def mm(a, b, ca, cb):
    return lax.dot_general(a, b, (((ca,), (cb,)), ((), ())), preferred_element_type=F32)


def row_sums(grad, out):
    product = grad.astype(F32) * out.astype(F32)
    high = product.astype(BF16)
    low = (product - high.astype(F32)).astype(BF16)
    ones = jnp.ones((8, HD), BF16)
    return mm(ones, high, 1, 1) + mm(ones, low, 1, 1)


def remote(src, dst, send, recv, device):
    return pltpu.make_async_remote_copy(
        src_ref=src, dst_ref=dst, send_sem=send, recv_sem=recv, device_id=device, device_id_type=MESH
    )


def arrived(dst, sem):
    pltpu.make_async_copy(dst, dst, sem).wait()


def push(src, dst, send, recv, device, here):
    @pl.when(here)
    def _():
        pltpu.make_async_copy(src, dst, recv).start()

    @pl.when(jnp.logical_not(here))
    def _():
        remote(src, dst, send, recv, device).start()


def pushed(src, dst, send, recv, device, here):
    @pl.when(jnp.logical_not(here))
    def _():
        remote(src, dst, send, recv, device).wait_send()


def kernel(
    eq, ek, ev, eo, ed, et, ck, cv, dq, do, dd, dt, es,
    raw, out_ck, out_cv, out_dq, out_w,
    es_v, ck_v, cv_v, dq_v, do_v, dd_v, dt_v, eo_v, ed_v, et_v, load_s,
    st_src, st_all, vg_all, z_src, z_recv, y_own, y_src, y_recv,
    kv, qd, stats_src, stats, acc, acc_recv, fin, dq_own, dq_send, dq_recv, dq_fin,
    dec_src, dec_recv, dec_mine, dec_other, dec_all,
    st_s, st_r, sty_s, stc_s, vg_s, vg_r, z_s, z_r, y_s, y_r,
    kv_s, kv_r, kvc_s, qd_s, qd_r, qdy_s, qdc_s, sta_s, sta_r, stay_s,
    acc_s, acc_r, fin_s, raw_r, dqy_s, dqy_r, dqo_s,
    dec_s, dec_r, decy_s, decy_r, deca_s, deca_r,
):
    z = lax.axis_index("dp")
    blk = lax.axis_index("blk")
    mp = lax.axis_index("mp")
    yh, x = blk // NX, blk % NX
    yl, c = mp // 2, mp % 2
    oyh, oyl, oc = 1 - yh, 1 - yl, 1 - c

    def dev(z_=None, yh_=None, x_=None, yl_=None, c_=None):
        z_ = z if z_ is None else z_
        yh_ = yh if yh_ is None else yh_
        x_ = x if x_ is None else x_
        yl_ = yl if yl_ is None else yl_
        c_ = c if c_ is None else c_
        return (z_, yh_ * NX + x_, yl_ * 2 + c_)

    def at_x(d):
        return (x + d) % NX

    sibling = dev(c_=oc)
    ylo = dev(yl_=oyl)
    yhi = dev(yh_=oyh)

    barrier = pltpu.get_barrier_semaphore()
    partners = [dev(x_=at_x(d), c_=(c + dc) % 2) for d in range(NX) for dc in range(2) if d or dc]
    partners += [yhi, ylo]
    partners += [dev(z_=(z + d) % NZ) for d in range(1, NZ)]
    for partner in partners:
        pl.semaphore_signal(barrier, inc=1, device_id=partner, device_id_type=MESH)

    loads = [pltpu.make_async_copy(src, dst, load_s.at[i]) for i, (src, dst) in enumerate(
        ((es, es_v), (ck, ck_v), (dq, dq_v), (dt, dt_v), (dd, dd_v), (cv, cv_v), (do, do_v),
         (eo, eo_v), (ed, ed_v), (et, et_v)))]
    for cp in loads:
        cp.start()

    loads[0].wait()
    for k in range(4):
        piece = es_v[0, :, k * 256:(k + 1) * 256].T
        st_src[k] = piece.reshape(NX, 64, 256)
    st_all[mp, x] = st_src[:, x]

    st_out = [remote(st_src.at[:, at_x(d)], st_all.at[mp, x], st_s.at[d], st_r.at[mp, x], dev(x_=at_x(d)))
              for d in (1, 3, 2)]

    def vg_to(e, s, d):
        return remote(vg_all.at[e, s], vg_all.at[e, s], vg_s.at[e, d], vg_r.at[e, s], dev(x_=at_x(d)))

    dec_out = [remote(dec_src.at[at_x(d)], dec_recv.at[x], dec_s.at[d], dec_r.at[x], dev(x_=at_x(d)))
               for d in (1, 3, 2)]
    def st_to_ylo(s):
        return remote(st_all.at[mp, s], st_all.at[mp, s], sty_s.at[s], st_r.at[mp, s], ylo)

    def st_to_sibling(m, k, s):
        return remote(st_all.at[m, s], st_all.at[m, s], stc_s.at[k, s], st_r.at[m, s], sibling)

    mine, other = mp, oyl * 2 + c
    enc_out, st_out_args = [], []
    for i in range(2):
        e = (x // 2 + i) % 2
        xt = c + 2 * e
        cols = pl.ds(pl.multiple_of(e * HD, HD), HD)
        for a, src in ((0, ek), (1, ev)):
            enc_out.append((src.at[0, :, cols], kv.at[a, x], kv_s.at[i, a], kv_r.at[a, x],
                            dev(x_=xt, c_=a), jnp.logical_and(xt == x, c == a), 0))
        here = jnp.logical_and(xt == x, c == yh)
        target = dev(x_=xt, c_=yh)
        for a, src in ((0, eq), (1, ed)):
            enc_out.append((src.at[0, :, cols], qd.at[0, x], qd_s.at[i, a], qd_r.at[0, x],
                            dev(x_=xt, c_=a), jnp.logical_and(xt == x, c == a), 1))
        st_out_args.append((stats_src.at[e], stats.at[x], sta_s.at[i], sta_r.at[x], target, here))

    qd_out, kv_out = [args for args in enc_out if args[6]], [args for args in enc_out if not args[6]]
    qd_out, kv_out = [args[:6] for args in qd_out], [args[:6] for args in kv_out]

    def send(some):
        for args in some:
            push(*args)

    cross = []

    def cross_values(e):
        if e == 0:
            for cp in loads[1:7]:
                cp.wait()
        cols = slice(e * HD, (e + 1) * HD)
        probs = jnp.exp(mm(ck_v[0, :, cols], dq_v[0, :, cols], 1, 1)) * (1.0 / dt_v[0, e:e + 1, :])
        value_grad = mm(probs.astype(BF16), dd_v[0, :, cols], 1, 0).astype(BF16)
        out_cv[0, :, cols] = value_grad
        vg_all[e, x] = value_grad
        cross.append(probs)

    def send_values(e):
        for d in (1, 3, 2):
            vg_to(e, x, d).start()

    def compute_stats():
        for cp in loads[7:]:
            cp.wait()
        for e in range(2):
            cols = slice(e * HD, (e + 1) * HD)
            stats_src[e, 0:4, :] = jnp.broadcast_to(1.0 / et_v[0, e:e + 1, :], (4, 256))
            stats_src[e, 4:8, :] = row_sums(ed_v[0, :, cols], eo_v[0, :, cols])[0:4, :]

    def cross_rest():
        for e in range(2):
            cols = slice(e * HD, (e + 1) * HD)
            keys, query, grad = ck_v[0, :, cols], dq_v[0, :, cols], dd_v[0, :, cols]
            delta = row_sums(grad, do_v[0, :, cols])[0:1, :]
            dscores = (cross[e] * (mm(cv_v[0, :, cols], grad, 1, 1) - delta)).astype(BF16)
            out_ck[0, :, cols] = mm(dscores, query, 1, 0).astype(BF16)
            dec_src[:, :, cols] = mm(dscores, keys, 0, 0).astype(BF16).reshape(NX, 64, HD)
        dec_recv[x] = dec_src[x]

    def states_step(d):
        s = at_x(d)
        arrived(st_all.at[mine, s], st_r.at[mine, s])
        st_to_ylo(s).start()
        st_to_sibling(mine, 0, s).start()

    def states_second():
        for d in ORDER:
            s = at_x(d)
            arrived(st_all.at[other, s], st_r.at[other, s])
            st_to_sibling(other, 1, s).start()

    def states_third():
        for s in range(NX):
            arrived(st_all.at[yl * 2 + oc, s], st_r.at[yl * 2 + oc, s])
            arrived(st_all.at[oyl * 2 + oc, s], st_r.at[oyl * 2 + oc, s])

    def value_arrives(e, d):
        arrived(vg_all.at[e, at_x(d)], vg_r.at[e, at_x(d)])

    def kv_to_sibling(s):
        return remote(kv.at[c, s], kv.at[c, s], kvc_s.at[s], kv_r.at[c, s], sibling)

    half = (c + yh) % 2

    def qd_to_yhi(s):
        return remote(qd.at[0, s], qd.at[1, s], qdy_s.at[s], qd_r.at[1, s], yhi)

    def qd_to_sibling(s):
        return remote(qd.at[1 - half, s], qd.at[2, s], qdc_s.at[s], qd_r.at[2, s], sibling)

    def stats_to_yhi(s):
        return remote(stats.at[s], stats.at[s], stay_s.at[s], sta_r.at[s], yhi)

    first_hand = c == yh

    dec_swap = remote(dec_mine, dec_other, decy_s, decy_r, yhi)
    z_out = []

    def decoder_sum():
        for d in (1, 3, 2):
            s = at_x(d)
            arrived(dec_recv.at[s], dec_r.at[s])
        total = dec_recv[0].astype(F32)
        for s in range(1, NX):
            total = total + dec_recv[s].astype(F32)
        dec_mine[...] = total
        dec_swap.start()

    def query_forward(d):
        s = at_x(d)
        arrived(qd.at[0, s], qd_r.at[0, s])
        qd_to_yhi(s).start()

        @pl.when(first_hand)
        def _():
            arrived(stats.at[s], sta_r.at[s])
            stats_to_yhi(s).start()

        @pl.when(jnp.logical_not(first_hand))
        def _():
            qd_to_sibling(s).start()

    def query_second(d):
        s = at_x(d)
        arrived(qd.at[1, s], qd_r.at[1, s])

        @pl.when(first_hand)
        def _():
            qd_to_sibling(s).start()

    def key_forward(d):
        s = at_x(d)
        arrived(kv.at[c, s], kv_r.at[c, s])
        kv_to_sibling(s).start()

    def queries_forward():
        for d in ORDER:
            query_forward(d)

    def keys_forward():
        for d in ORDER:
            key_forward(d)

    def weight_gradient(e):
        for m in range(4):
            part = mm(st_all[m, 0].reshape(256, 256), vg_all[e, 0], 1, 0)
            for s in range(1, NX):
                part = part + mm(st_all[m, s].reshape(256, 256), vg_all[e, s], 1, 0)
            z_src[e, 2 * m:2 * m + 2] = part.astype(BF16).reshape(2, 128, HD)
        z_recv[e, z] = z_src[e, z]
        for d in (4, 3, 5, 2, 6, 1, 7):
            zt = (z + d) % NZ
            cp = remote(z_src.at[e, zt], z_recv.at[e, z], z_s.at[e, d], z_r.at[e, z], dev(z_=zt))
            cp.start()
            z_out.append(cp)

    pl.semaphore_wait(barrier, len(partners))

    def own():
        st_to_ylo(x).start()
        st_to_sibling(mine, 0, x).start()

    deca_out = []

    def decoder_out():
        dec_swap.wait()
        dec_all[x] = (dec_mine[...] + dec_other[...]).astype(BF16)
        for d in (1, 3, 2):
            cp = remote(dec_all.at[x], dec_all.at[x], deca_s.at[d], deca_r.at[x], dev(x_=at_x(d)))
            cp.start()
            deca_out.append(cp)

    def start(copies):
        for cp in copies:
            cp.start()

    start(st_out[:2])
    own()
    start(st_out[2:])
    cross_values(0)
    compute_stats()
    send(qd_out)
    send(st_out_args)
    states_step(1)
    states_step(3)
    states_step(2)
    cross_values(1)
    send_values(0)
    send(kv_out)
    cross_rest()
    queries_forward()
    states_second()
    value_arrives(0, 1)
    value_arrives(0, 3)
    value_arrives(0, 2)
    states_third()
    weight_gradient(0)
    keys_forward()
    send_values(1)
    start(dec_out)

    for s in range(NX):
        arrived(kv.at[oc, s], kv_r.at[oc, s])

    def dq_to_yhi(s):
        return remote(dq_send.at[s], dq_recv.at[s], dqy_s.at[s], dqy_r.at[s], yhi)

    def acc_to_sibling(b):
        return remote(acc.at[oc, b], acc_recv.at[b], acc_s.at[b], acc_r.at[b], sibling)

    for i, d in enumerate(ORDER):
        s = at_x(d)

        query_second(d)

        @pl.when(jnp.logical_not(first_hand))
        def _(s=s):
            arrived(stats.at[s], sta_r.at[s])

        arrived(qd.at[2, s], qd_r.at[2, s])
        query, grad = qd[half * (1 - c) + 2 * c, s], qd[half * c + 2 * (1 - c), s]
        inv, delta = stats[s, 0:1, :], stats[s, 4:5, :]
        grad_q = jnp.zeros((256, HD), F32)
        for h in range(2):
            keys = kv[0, 2 * h:2 * h + 2].reshape(512, HD)
            vals = kv[1, 2 * h:2 * h + 2].reshape(512, HD)
            probs = jnp.exp(mm(keys, query, 1, 1)) * inv
            weights = probs.astype(BF16)
            dscores = (probs * (mm(vals, grad, 1, 1) - delta)).astype(BF16)
            value_part = mm(weights, grad, 1, 0).reshape(2, 256, HD)
            key_part = mm(dscores, query, 1, 0).reshape(2, 256, HD)
            grad_q = grad_q + mm(dscores, keys, 0, 0)
            if i:
                key_part = key_part + acc[0, 2 * h:2 * h + 2]
                value_part = value_part + acc[1, 2 * h:2 * h + 2]
            acc[0, 2 * h:2 * h + 2] = key_part
            acc[1, 2 * h:2 * h + 2] = value_part
            if i == NX - 1:
                for b in (2 * h, 2 * h + 1):
                    acc_to_sibling(b).start()

        @pl.when(first_hand)
        def _(s=s, grad_q=grad_q):
            dq_own[s] = grad_q

        @pl.when(jnp.logical_not(first_hand))
        def _(s=s, grad_q=grad_q):
            dq_send[s] = grad_q.astype(BF16)
            dq_to_yhi(s).start()

    e_of = x // 2
    owner_c = x % 2
    fin_out = []

    def keys_back():
        for b in range(NX):
            arrived(acc_recv.at[b], acc_r.at[b])
            fin[b] = (acc[c, b] + acc_recv[b]).astype(BF16)
            args = (fin.at[b], raw.at[c, e_of], fin_s.at[b], raw_r.at[c, e_of], dev(x_=b, c_=owner_c),
                    jnp.logical_and(b == x, c == owner_c))
            push(*args)
            fin_out.append(args)

    def dq_args(s):
        return (dq_fin.at[s], raw.at[2, e_of], dqo_s.at[s], raw_r.at[2, e_of], dev(x_=s, c_=owner_c),
                jnp.logical_and(s == x, c == owner_c))

    def queries_back():
        @pl.when(first_hand)
        def _():
            for d in ORDER:
                s = at_x(d)
                arrived(dq_recv.at[s], dqy_r.at[s])
                dq_fin[s] = (dq_own[s] + dq_recv[s].astype(F32)).astype(BF16)
                push(*dq_args(s))

    keys_back()
    queries_back()
    value_arrives(1, 1)
    value_arrives(1, 3)
    value_arrives(1, 2)
    weight_gradient(1)
    decoder_sum()
    decoder_out()

    def y_swap(e):
        return remote(y_src.at[e, oyh], y_recv.at[e], y_s.at[e], y_r.at[e], yhi)

    for e in range(2):
        for d in (1, 7, 2, 6, 3, 5, 4):
            s = (z + d) % NZ
            arrived(z_recv.at[e, s], z_r.at[e, s])
        w = z_recv[e, 0].astype(F32)
        for s in range(1, NZ):
            w = w + z_recv[e, s].astype(F32)
        w = w.reshape(2, 64, HD)
        y_own[e] = w
        y_src[e] = w.astype(y_src.dtype)
        y_swap(e).start()

    for d in (1, 3, 2):
        s = at_x(d)
        arrived(dec_all.at[s], deca_r.at[s])
    out_dq[0] = dec_all[...].reshape(256, 512)

    for e in range(2):
        for a in range(3):
            arrived(raw.at[a, e], raw_r.at[a, e])

    for e in range(2):
        y_swap(e).wait()
        out_w[:, e * HD:(e + 1) * HD] = y_own[e, yh] + y_recv[e].astype(F32)

    for cp in st_out + dec_out + deca_out + z_out:
        cp.wait_send()
    for d in range(NX):
        st_to_ylo(d).wait_send()
        st_to_sibling(mine, 0, d).wait_send()
        st_to_sibling(other, 1, d).wait_send()
        kv_to_sibling(d).wait_send()
        acc_to_sibling(d).wait_send()
    for e in range(2):
        for d in (1, 3, 2):
            vg_to(e, x, d).wait_send()
    for args in qd_out + kv_out + st_out_args + fin_out:
        pushed(*args)

    for s in range(NX):
        qd_to_yhi(s).wait_send()
        qd_to_sibling(s).wait_send()

    @pl.when(first_hand)
    def _():
        for s in range(NX):
            stats_to_yhi(s).wait_send()
            pushed(*dq_args(s))

    @pl.when(jnp.logical_not(first_hand))
    def _():
        for s in range(NX):
            dq_to_yhi(s).wait_send()


def finish(raw, in_ck, in_cv, in_dq, in_w, out_q, out_k, out_v, out_ck, out_cv, out_dq, out_w, sems):
    copies = []
    for a, out in ((0, out_k), (1, out_v), (2, out_q)):
        for e in range(2):
            copies.append((raw.at[a, e], out.at[0, :, e * HD:(e + 1) * HD]))
    copies += [(in_ck, out_ck), (in_cv, out_cv), (in_dq, out_dq), (in_w, out_w)]
    copies = [pltpu.make_async_copy(src, dst, sems.at[i]) for i, (src, dst) in enumerate(copies)]
    for cp in copies:
        cp.start()
    for cp in copies:
        cp.wait()


def body(*arrays):
    hbm = pl.BlockSpec(memory_space=pltpu.HBM)
    vmem = pl.BlockSpec(memory_space=pltpu.VMEM)
    dma = pltpu.SemaphoreType.DMA
    grads = [((1, 256, 512), BF16)] * 3 + [((64, 512), F32)]
    outs = [pltpu.VMEM((3, 2, 256, HD), BF16)] + [pltpu.VMEM(shape, dtype) for shape, dtype in grads]
    buffers = [((1, 256, 1024), BF16)] + [((1, 256, 512), BF16)] * 5 + [((1, 2, 256), F32)]
    buffers += [((1, 256, 512), BF16)] * 2 + [((1, 2, 256), F32)]
    scratch = [pltpu.VMEM(shape, dtype) for shape, dtype in buffers] + [dma((10,))]
    buffers = [
        ((4, NX, 64, 256), BF16), ((4, NX, 4, 64, 256), BF16), ((2, NX, 256, HD), BF16),
        ((2, NZ, 128, HD), BF16), ((2, NZ, 128, HD), BF16), ((2, 2, 64, HD), F32), ((2, 2, 64, HD), SWAP),
        ((2, 64, HD), SWAP),
        ((2, NX, 256, HD), BF16), ((3, NX, 256, HD), BF16), ((2, 8, 256), F32), ((NX, 8, 256), F32),
        ((2, NX, 256, HD), F32), ((NX, 256, HD), F32), ((NX, 256, HD), BF16), ((NX, 256, HD), F32),
        ((NX, 256, HD), BF16), ((NX, 256, HD), BF16), ((NX, 256, HD), BF16),
        ((NX, 64, 512), BF16), ((NX, 64, 512), BF16), ((64, 512), F32), ((64, 512), F32), ((NX, 64, 512), BF16),
    ]
    semaphores = [
        (NX,), (4, NX), (NX,), (2, NX), (2, NX), (2, NX), (2, NZ), (2, NZ), (2,), (2,),
        (2, 2), (2, NX), (NX,), (2, 2), (3, NX), (NX,), (NX,), (2,), (NX,), (NX,),
        (NX,), (NX,), (NX,), (3, 2), (NX,), (NX,), (NX,),
        (NX,), (NX,), None, None, (NX,), (NX,),
    ]
    scratch += [pltpu.VMEM(*buffer) for buffer in buffers]
    scratch += [dma if shape is None else dma(shape) for shape in semaphores]
    parts = pl.pallas_call(
        kernel,
        out_shape=outs,
        in_specs=[hbm] * 13,
        out_specs=[vmem] * 5,
        scratch_shapes=scratch,
        compiler_params=pltpu.CompilerParams(
            collective_id=0, has_side_effects=True, vmem_limit_bytes=40 * 1024 * 1024
        ),
        cost_estimate=pl.CostEstimate(flops=5_000_000_000, bytes_accessed=6_000_000, transcendentals=1_200_000),
        name="grads",
    )(*[pltpu.with_memory_space_constraint(array, pltpu.HBM) for array in arrays])
    shapes = [jax.ShapeDtypeStruct(shape, dtype) for shape, dtype in [((1, 256, 512), BF16)] * 3 + grads]
    return tuple(pl.pallas_call(
        finish,
        out_shape=shapes,
        in_specs=[vmem] * 5,
        out_specs=[hbm] * 7,
        scratch_shapes=[dma((10,))],
        compiler_params=pltpu.CompilerParams(vmem_limit_bytes=2 * 1024 * 1024),
        name="finish",
    )(*[pltpu.with_memory_space_constraint(part, pltpu.VMEM) for part in parts]))


def solution(mesh):
    rows = P("dp", "blk", "mp")
    tokens = P("dp", None, "mp")
    in_specs = (rows, rows, rows, rows, rows, P("dp", "mp", "blk"), rows, rows, tokens, tokens, tokens,
                P("dp", "mp", None), rows)
    out_specs = (rows, rows, rows, rows, rows, tokens, P(("dp", "blk"), "mp"))
    return jax.shard_map(body, mesh=mesh, in_specs=in_specs, out_specs=out_specs, check_vma=False)
```

```python
import jax
import jax.numpy as jnp
from jax import lax
from jax.experimental import pallas as pl
from jax.experimental.pallas import tpu as pltpu
from jax.sharding import PartitionSpec as P

HD = 256
NX = 4
NZ = 8
F32 = jnp.float32
BF16 = jnp.bfloat16
MESH = pl.DeviceIdType.MESH
ORDER = (0, 1, 3, 2)


def mm(a, b, ca, cb):
    return lax.dot_general(a, b, (((ca,), (cb,)), ((), ())), preferred_element_type=F32)


def row_sums(grad, out):
    product = grad.astype(F32) * out.astype(F32)
    high = product.astype(BF16)
    low = (product - high.astype(F32)).astype(BF16)
    ones = jnp.ones((8, HD), BF16)
    return mm(ones, high, 1, 1) + mm(ones, low, 1, 1)


def remote(src, dst, send, recv, device):
    return pltpu.make_async_remote_copy(
        src_ref=src, dst_ref=dst, send_sem=send, recv_sem=recv, device_id=device, device_id_type=MESH
    )


def arrived(dst, sem):
    pltpu.make_async_copy(dst, dst, sem).wait()


def push(src, dst, send, recv, device, here):
    @pl.when(here)
    def _():
        pltpu.make_async_copy(src, dst, recv).start()

    @pl.when(jnp.logical_not(here))
    def _():
        remote(src, dst, send, recv, device).start()


def pushed(src, dst, send, recv, device, here):
    @pl.when(jnp.logical_not(here))
    def _():
        remote(src, dst, send, recv, device).wait_send()


def kernel(
    eq, ek, ev, eo, ed, et, ck, cv, dq, do, dd, dt, es,
    raw, out_ck, out_cv, out_dq, out_w,
    es_v, ck_v, cv_v, dq_v, do_v, dd_v, dt_v, eo_v, ed_v, et_v, load_s,
    st_src, st_all, vg_all, z_src, z_recv, y_own, y_src, y_recv,
    kv, qd, stats_src, stats, acc, acc_recv, fin, dq_own, dq_send, dq_recv, dq_fin,
    dec_src, dec_recv, dec_mine, dec_other, dec_all,
    st_s, st_r, sty_s, stc_s, vg_s, vg_r, z_s, z_r, y_s, y_r,
    kv_s, kv_r, kvc_s, qd_s, qd_r, qdy_s, qdc_s, sta_s, sta_r, stay_s,
    acc_s, acc_r, fin_s, raw_r, dqy_s, dqy_r, dqo_s,
    dec_s, dec_r, decy_s, decy_r, deca_s, deca_r, near,
):
    z = lax.axis_index("dp")
    blk = lax.axis_index("blk")
    mp = lax.axis_index("mp")
    yh, x = blk // NX, blk % NX
    yl, c = mp // 2, mp % 2
    oyh, oyl, oc = 1 - yh, 1 - yl, 1 - c

    def dev(z_=None, yh_=None, x_=None, yl_=None, c_=None):
        z_ = z if z_ is None else z_
        yh_ = yh if yh_ is None else yh_
        x_ = x if x_ is None else x_
        yl_ = yl if yl_ is None else yl_
        c_ = c if c_ is None else c_
        return (z_, yh_ * NX + x_, yl_ * 2 + c_)

    def at_x(d):
        return (x + d) % NX

    sibling = dev(c_=oc)
    ylo = dev(yl_=oyl)
    yhi = dev(yh_=oyh)

    barrier = pltpu.get_barrier_semaphore()
    partners = [dev(x_=at_x(d), c_=(c + dc) % 2) for d in range(NX) for dc in range(2) if d or dc]
    partners += [yhi, ylo]
    partners += [dev(z_=(z + d) % NZ) for d in (1, NZ - 1)]
    for partner in partners:
        pl.semaphore_signal(barrier, inc=1, device_id=partner, device_id_type=MESH)

    loads = [pltpu.make_async_copy(src, dst, load_s.at[i]) for i, (src, dst) in enumerate(
        ((es, es_v), (ck, ck_v), (dq, dq_v), (dt, dt_v), (dd, dd_v), (cv, cv_v), (do, do_v),
         (eo, eo_v), (ed, ed_v), (et, et_v)))]
    for cp in loads:
        cp.start()

    loads[0].wait()
    for k in range(4):
        piece = es_v[0, :, k * 256:(k + 1) * 256].T
        st_src[k] = piece.reshape(NX, 64, 256)
    st_all[mp, x] = st_src[:, x]

    st_out = [remote(st_src.at[:, at_x(d)], st_all.at[mp, x], st_s.at[d], st_r.at[mp, x], dev(x_=at_x(d)))
              for d in (1, 3, 2)]

    def vg_to(e, s, d):
        return remote(vg_all.at[e, s], vg_all.at[e, s], vg_s.at[e, d], vg_r.at[e, s], dev(x_=at_x(d)))

    dec_out = [remote(dec_src.at[at_x(d)], dec_recv.at[x], dec_s.at[d], dec_r.at[x], dev(x_=at_x(d)))
               for d in (1, 3, 2)]
    def st_to_ylo(s):
        return remote(st_all.at[mp, s], st_all.at[mp, s], sty_s.at[s], st_r.at[mp, s], ylo)

    def st_to_sibling(m, k, s):
        return remote(st_all.at[m, s], st_all.at[m, s], stc_s.at[k, s], st_r.at[m, s], sibling)

    mine, other = mp, oyl * 2 + c
    enc_out, st_out_args = [], []
    for i in range(2):
        e = (x // 2 + i) % 2
        xt = c + 2 * e
        cols = pl.ds(pl.multiple_of(e * HD, HD), HD)
        for a, src in ((0, ek), (1, ev)):
            enc_out.append((src.at[0, :, cols], kv.at[a, x], kv_s.at[i, a], kv_r.at[a, x],
                            dev(x_=xt, c_=a), jnp.logical_and(xt == x, c == a), 0))
        here = jnp.logical_and(xt == x, c == yh)
        target = dev(x_=xt, c_=yh)
        for a, src in ((0, eq), (1, ed)):
            enc_out.append((src.at[0, :, cols], qd.at[0, x], qd_s.at[i, a], qd_r.at[0, x],
                            dev(x_=xt, c_=a), jnp.logical_and(xt == x, c == a), 1))
        st_out_args.append((stats_src.at[e], stats.at[x], sta_s.at[i], sta_r.at[x], target, here))

    qd_out, kv_out = [args for args in enc_out if args[6]], [args for args in enc_out if not args[6]]
    qd_out, kv_out = [args[:6] for args in qd_out], [args[:6] for args in kv_out]

    def send(some):
        for args in some:
            push(*args)

    cross = []

    def cross_values(e):
        if e == 0:
            for cp in loads[1:7]:
                cp.wait()
        cols = slice(e * HD, (e + 1) * HD)
        probs = jnp.exp(mm(ck_v[0, :, cols], dq_v[0, :, cols], 1, 1)) * (1.0 / dt_v[0, e:e + 1, :])
        value_grad = mm(probs.astype(BF16), dd_v[0, :, cols], 1, 0).astype(BF16)
        out_cv[0, :, cols] = value_grad
        vg_all[e, x] = value_grad
        cross.append(probs)

    def send_values(e):
        for d in (1, 3, 2):
            vg_to(e, x, d).start()

    def compute_stats():
        for cp in loads[7:]:
            cp.wait()
        for e in range(2):
            cols = slice(e * HD, (e + 1) * HD)
            stats_src[e, 0:4, :] = jnp.broadcast_to(1.0 / et_v[0, e:e + 1, :], (4, 256))
            stats_src[e, 4:8, :] = row_sums(ed_v[0, :, cols], eo_v[0, :, cols])[0:4, :]

    def cross_rest():
        for e in range(2):
            cols = slice(e * HD, (e + 1) * HD)
            keys, query, grad = ck_v[0, :, cols], dq_v[0, :, cols], dd_v[0, :, cols]
            delta = row_sums(grad, do_v[0, :, cols])[0:1, :]
            dscores = (cross[e] * (mm(cv_v[0, :, cols], grad, 1, 1) - delta)).astype(BF16)
            out_ck[0, :, cols] = mm(dscores, query, 1, 0).astype(BF16)
            dec_src[:, :, cols] = mm(dscores, keys, 0, 0).astype(BF16).reshape(NX, 64, HD)
        dec_recv[x] = dec_src[x]

    def states_step(d):
        s = at_x(d)
        arrived(st_all.at[mine, s], st_r.at[mine, s])
        st_to_ylo(s).start()
        st_to_sibling(mine, 0, s).start()

    def states_second():
        for d in ORDER:
            s = at_x(d)
            arrived(st_all.at[other, s], st_r.at[other, s])
            st_to_sibling(other, 1, s).start()

    def states_third():
        for s in range(NX):
            arrived(st_all.at[yl * 2 + oc, s], st_r.at[yl * 2 + oc, s])
            arrived(st_all.at[oyl * 2 + oc, s], st_r.at[oyl * 2 + oc, s])

    def value_arrives(e, d):
        arrived(vg_all.at[e, at_x(d)], vg_r.at[e, at_x(d)])

    def kv_to_sibling(s):
        return remote(kv.at[c, s], kv.at[c, s], kvc_s.at[s], kv_r.at[c, s], sibling)

    half = (c + yh) % 2

    def qd_to_yhi(s):
        return remote(qd.at[0, s], qd.at[1, s], qdy_s.at[s], qd_r.at[1, s], yhi)

    def qd_to_sibling(s):
        return remote(qd.at[1 - half, s], qd.at[2, s], qdc_s.at[s], qd_r.at[2, s], sibling)

    def stats_to_yhi(s):
        return remote(stats.at[s], stats.at[s], stay_s.at[s], sta_r.at[s], yhi)

    first_hand = c == yh

    dec_swap = remote(dec_mine, dec_other, decy_s, decy_r, yhi)
    z_out = []

    def decoder_sum():
        for d in (1, 3, 2):
            s = at_x(d)
            arrived(dec_recv.at[s], dec_r.at[s])
        total = dec_recv[0].astype(F32)
        for s in range(1, NX):
            total = total + dec_recv[s].astype(F32)
        dec_mine[...] = total
        dec_swap.start()

    def query_forward(d):
        s = at_x(d)
        arrived(qd.at[0, s], qd_r.at[0, s])
        qd_to_yhi(s).start()

        @pl.when(first_hand)
        def _():
            arrived(stats.at[s], sta_r.at[s])
            stats_to_yhi(s).start()

        @pl.when(jnp.logical_not(first_hand))
        def _():
            qd_to_sibling(s).start()

    def query_second(d):
        s = at_x(d)
        arrived(qd.at[1, s], qd_r.at[1, s])

        @pl.when(first_hand)
        def _():
            qd_to_sibling(s).start()

    def key_forward(d):
        s = at_x(d)
        arrived(kv.at[c, s], kv_r.at[c, s])
        kv_to_sibling(s).start()

    def queries_forward():
        for d in ORDER:
            query_forward(d)

    def keys_forward():
        for d in ORDER:
            key_forward(d)

    def weight_gradient(e):
        for m in range(4):
            part = mm(st_all[m, 0].reshape(256, 256), vg_all[e, 0], 1, 0)
            for s in range(1, NX):
                part = part + mm(st_all[m, s].reshape(256, 256), vg_all[e, s], 1, 0)
            z_src[e, 2 * m:2 * m + 2] = part.astype(BF16).reshape(2, 128, HD)
        z_recv[e, z] = z_src[e, z]
        for d in (4, 3, 5, 2, 6, 1, 7):
            zt = (z + d) % NZ
            cp = remote(z_src.at[e, zt], z_recv.at[e, z], z_s.at[e, d], z_r.at[e, z], dev(z_=zt))
            cp.start()
            z_out.append(cp)

    pl.semaphore_wait(barrier, len(partners))

    def greet():
        for way, d in ((0, 1), (1, NZ - 1)):
            pl.semaphore_signal(near.at[way], inc=1, device_id=dev(z_=(z + d) % NZ), device_id_type=MESH)

    def greeted():
        for way in range(2):
            pl.semaphore_wait(near.at[way], 1)

    def own():
        st_to_ylo(x).start()
        st_to_sibling(mine, 0, x).start()

    deca_out = []

    def decoder_out():
        dec_swap.wait()
        dec_all[x] = (dec_mine[...] + dec_other[...]).astype(BF16)
        for d in (1, 3, 2):
            cp = remote(dec_all.at[x], dec_all.at[x], deca_s.at[d], deca_r.at[x], dev(x_=at_x(d)))
            cp.start()
            deca_out.append(cp)

    def start(copies):
        for cp in copies:
            cp.start()

    start(st_out[:2])
    own()
    start(st_out[2:])
    greet()
    cross_values(0)
    compute_stats()
    send(qd_out)
    send(st_out_args)
    greeted()
    greet()
    states_step(1)
    states_step(3)
    states_step(2)
    cross_values(1)
    send_values(0)
    greeted()
    greet()
    send(kv_out)
    cross_rest()
    queries_forward()
    states_second()
    greeted()
    value_arrives(0, 1)
    value_arrives(0, 3)
    value_arrives(0, 2)
    states_third()
    weight_gradient(0)
    keys_forward()
    send_values(1)
    start(dec_out)

    for s in range(NX):
        arrived(kv.at[oc, s], kv_r.at[oc, s])

    def dq_to_yhi(s):
        return remote(dq_send.at[s], dq_recv.at[s], dqy_s.at[s], dqy_r.at[s], yhi)

    def acc_to_sibling(b):
        return remote(acc.at[oc, b], acc_recv.at[b], acc_s.at[b], acc_r.at[b], sibling)

    for i, d in enumerate(ORDER):
        s = at_x(d)

        query_second(d)

        @pl.when(jnp.logical_not(first_hand))
        def _(s=s):
            arrived(stats.at[s], sta_r.at[s])

        arrived(qd.at[2, s], qd_r.at[2, s])
        query, grad = qd[half * (1 - c) + 2 * c, s], qd[half * c + 2 * (1 - c), s]
        inv, delta = stats[s, 0:1, :], stats[s, 4:5, :]
        grad_q = jnp.zeros((256, HD), F32)
        for h in range(2):
            keys = kv[0, 2 * h:2 * h + 2].reshape(512, HD)
            vals = kv[1, 2 * h:2 * h + 2].reshape(512, HD)
            probs = jnp.exp(mm(keys, query, 1, 1)) * inv
            weights = probs.astype(BF16)
            dscores = (probs * (mm(vals, grad, 1, 1) - delta)).astype(BF16)
            value_part = mm(weights, grad, 1, 0).reshape(2, 256, HD)
            key_part = mm(dscores, query, 1, 0).reshape(2, 256, HD)
            grad_q = grad_q + mm(dscores, keys, 0, 0)
            if i:
                key_part = key_part + acc[0, 2 * h:2 * h + 2]
                value_part = value_part + acc[1, 2 * h:2 * h + 2]
            acc[0, 2 * h:2 * h + 2] = key_part
            acc[1, 2 * h:2 * h + 2] = value_part
            if i == NX - 1:
                for b in (2 * h, 2 * h + 1):
                    acc_to_sibling(b).start()

        @pl.when(first_hand)
        def _(s=s, grad_q=grad_q):
            dq_own[s] = grad_q

        @pl.when(jnp.logical_not(first_hand))
        def _(s=s, grad_q=grad_q):
            dq_send[s] = grad_q.astype(BF16)
            dq_to_yhi(s).start()

    e_of = x // 2
    owner_c = x % 2
    fin_out = []

    def keys_back():
        for b in range(NX):
            arrived(acc_recv.at[b], acc_r.at[b])
            fin[b] = (acc[c, b] + acc_recv[b]).astype(BF16)
            args = (fin.at[b], raw.at[c, e_of], fin_s.at[b], raw_r.at[c, e_of], dev(x_=b, c_=owner_c),
                    jnp.logical_and(b == x, c == owner_c))
            push(*args)
            fin_out.append(args)

    def dq_args(s):
        return (dq_fin.at[s], raw.at[2, e_of], dqo_s.at[s], raw_r.at[2, e_of], dev(x_=s, c_=owner_c),
                jnp.logical_and(s == x, c == owner_c))

    def queries_back():
        @pl.when(first_hand)
        def _():
            for d in ORDER:
                s = at_x(d)
                arrived(dq_recv.at[s], dqy_r.at[s])
                dq_fin[s] = (dq_own[s] + dq_recv[s].astype(F32)).astype(BF16)
                push(*dq_args(s))

    keys_back()
    queries_back()
    value_arrives(1, 1)
    value_arrives(1, 3)
    value_arrives(1, 2)
    weight_gradient(1)
    decoder_sum()
    decoder_out()

    def y_swap(e):
        return remote(y_src.at[e, oyh], y_recv.at[e], y_s.at[e], y_r.at[e], yhi)

    for e in range(2):
        for d in (1, 7, 2, 6, 3, 5, 4):
            s = (z + d) % NZ
            arrived(z_recv.at[e, s], z_r.at[e, s])
        w = z_recv[e, 0].astype(F32)
        for s in range(1, NZ):
            w = w + z_recv[e, s].astype(F32)
        w = w.reshape(2, 64, HD)
        y_own[e] = w
        y_src[e] = w.astype(y_src.dtype)
        y_swap(e).start()

    for d in (1, 3, 2):
        s = at_x(d)
        arrived(dec_all.at[s], deca_r.at[s])
    out_dq[0] = dec_all[...].reshape(256, 512)

    for e in range(2):
        for a in range(3):
            arrived(raw.at[a, e], raw_r.at[a, e])

    for e in range(2):
        y_swap(e).wait()
        out_w[:, e * HD:(e + 1) * HD] = y_own[e, yh] + y_recv[e].astype(F32)

    for cp in st_out + dec_out + deca_out + z_out:
        cp.wait_send()
    for d in range(NX):
        st_to_ylo(d).wait_send()
        st_to_sibling(mine, 0, d).wait_send()
        st_to_sibling(other, 1, d).wait_send()
        kv_to_sibling(d).wait_send()
        acc_to_sibling(d).wait_send()
    for e in range(2):
        for d in (1, 3, 2):
            vg_to(e, x, d).wait_send()
    for args in qd_out + kv_out + st_out_args + fin_out:
        pushed(*args)

    for s in range(NX):
        qd_to_yhi(s).wait_send()
        qd_to_sibling(s).wait_send()

    @pl.when(first_hand)
    def _():
        for s in range(NX):
            stats_to_yhi(s).wait_send()
            pushed(*dq_args(s))

    @pl.when(jnp.logical_not(first_hand))
    def _():
        for s in range(NX):
            dq_to_yhi(s).wait_send()


def finish(raw, in_ck, in_cv, in_dq, in_w, out_q, out_k, out_v, out_ck, out_cv, out_dq, out_w, sems):
    copies = []
    for a, out in ((0, out_k), (1, out_v), (2, out_q)):
        for e in range(2):
            copies.append((raw.at[a, e], out.at[0, :, e * HD:(e + 1) * HD]))
    copies += [(in_ck, out_ck), (in_cv, out_cv), (in_dq, out_dq), (in_w, out_w)]
    copies = [pltpu.make_async_copy(src, dst, sems.at[i]) for i, (src, dst) in enumerate(copies)]
    for cp in copies:
        cp.start()
    for cp in copies:
        cp.wait()


def body(*arrays):
    hbm = pl.BlockSpec(memory_space=pltpu.HBM)
    vmem = pl.BlockSpec(memory_space=pltpu.VMEM)
    dma = pltpu.SemaphoreType.DMA
    grads = [((1, 256, 512), BF16)] * 3 + [((64, 512), F32)]
    outs = [pltpu.VMEM((3, 2, 256, HD), BF16)] + [pltpu.VMEM(shape, dtype) for shape, dtype in grads]
    buffers = [((1, 256, 1024), BF16)] + [((1, 256, 512), BF16)] * 5 + [((1, 2, 256), F32)]
    buffers += [((1, 256, 512), BF16)] * 2 + [((1, 2, 256), F32)]
    scratch = [pltpu.VMEM(shape, dtype) for shape, dtype in buffers] + [dma((10,))]
    buffers = [
        ((4, NX, 64, 256), BF16), ((4, NX, 4, 64, 256), BF16), ((2, NX, 256, HD), BF16),
        ((2, NZ, 128, HD), BF16), ((2, NZ, 128, HD), BF16), ((2, 2, 64, HD), F32), ((2, 2, 64, HD), F32),
        ((2, 64, HD), F32),
        ((2, NX, 256, HD), BF16), ((3, NX, 256, HD), BF16), ((2, 8, 256), F32), ((NX, 8, 256), F32),
        ((2, NX, 256, HD), F32), ((NX, 256, HD), F32), ((NX, 256, HD), BF16), ((NX, 256, HD), F32),
        ((NX, 256, HD), BF16), ((NX, 256, HD), BF16), ((NX, 256, HD), BF16),
        ((NX, 64, 512), BF16), ((NX, 64, 512), BF16), ((64, 512), F32), ((64, 512), F32), ((NX, 64, 512), BF16),
    ]
    semaphores = [
        (NX,), (4, NX), (NX,), (2, NX), (2, NX), (2, NX), (2, NZ), (2, NZ), (2,), (2,),
        (2, 2), (2, NX), (NX,), (2, 2), (3, NX), (NX,), (NX,), (2,), (NX,), (NX,),
        (NX,), (NX,), (NX,), (3, 2), (NX,), (NX,), (NX,),
        (NX,), (NX,), None, None, (NX,), (NX,),
    ]
    scratch += [pltpu.VMEM(*buffer) for buffer in buffers]
    scratch += [dma if shape is None else dma(shape) for shape in semaphores]
    scratch += [pltpu.SemaphoreType.REGULAR((2,))]
    parts = pl.pallas_call(
        kernel,
        out_shape=outs,
        in_specs=[hbm] * 13,
        out_specs=[vmem] * 5,
        scratch_shapes=scratch,
        compiler_params=pltpu.CompilerParams(
            collective_id=0, has_side_effects=True, vmem_limit_bytes=40 * 1024 * 1024
        ),
        cost_estimate=pl.CostEstimate(flops=5_000_000_000, bytes_accessed=6_000_000, transcendentals=1_200_000),
        name="grads",
    )(*[pltpu.with_memory_space_constraint(array, pltpu.HBM) for array in arrays])
    shapes = [jax.ShapeDtypeStruct(shape, dtype) for shape, dtype in [((1, 256, 512), BF16)] * 3 + grads]
    return tuple(pl.pallas_call(
        finish,
        out_shape=shapes,
        in_specs=[vmem] * 5,
        out_specs=[hbm] * 7,
        scratch_shapes=[dma((10,))],
        compiler_params=pltpu.CompilerParams(vmem_limit_bytes=2 * 1024 * 1024),
        name="finish",
    )(*[pltpu.with_memory_space_constraint(part, pltpu.VMEM) for part in parts]))


def solution(mesh):
    rows = P("dp", "blk", "mp")
    tokens = P("dp", None, "mp")
    in_specs = (rows, rows, rows, rows, rows, P("dp", "mp", "blk"), rows, rows, tokens, tokens, tokens,
                P("dp", "mp", None), rows)
    out_specs = (rows, rows, rows, rows, rows, tokens, P(("dp", "blk"), "mp"))
    return jax.shard_map(body, mesh=mesh, in_specs=in_specs, out_specs=out_specs, check_vma=False)
```
